32 devices in a mesh: dp: 16 (over z, x, core), group: 2 (over y).
Axes of the slice: x: 2, y: 2, z: 4, core: 2. Of those that a mesh axis runs over, the one named last changes fastest.
Arguments:
- queries: bfloat16 [4096, 256], P('dp'), may hold values from -110 to 110
- item_features: bfloat16 [4096, 2048], P('dp', 'group'), may hold values from -6 to 6
- corpus: bfloat16 [32768, 2048], P('dp', 'group'), may hold values from -6 to 6
- sample_ids: int32 [16384], P('dp'), may hold values from 0 to 2047
- sample_shift: bfloat16 [16384], P('dp'), may hold values from -2 to 2
- w1: bfloat16 [2048, 1024], P(None, 'group'), may hold values from -0.125 to 0.125
- w2: bfloat16 [1024, 256], P('group'), may hold values from -0.1875 to 0.1875
Outputs:
- query_loss: float32 [4096], P(('dp', 'group'))
- grad_query: float32 [4096, 256], P(('dp', 'group'))
- grad_w1: float32 [2048, 1024], P(None, 'group')
- grad_w2: float32 [1024, 256], P('group')
The draws below stay inside these ranges and needn't reach their ends.
Inputs may be any that keep to these rules, and one draw needn't show every extreme that they name: sample_ids[k] is a row of the corpus block of the dp index that holds position k.
All inputs are finite; a program needn't handle non-finite values.
Results may differ from the reference program's by a relative error of at most 0.02.
The reference program's roundings to bfloat16 on the way count: a program that leaves them out, or rounds other values in their place, can miss the bound.
Values may be sent and summed in bfloat16 or wider, within the bound.
A program may use at most 128 MiB of HBM per device.

```python
import math
import jax
import jax.numpy as jnp
from jax import lax

F = 2048
H = 1024
E = 256
Q_DP = 256
NEG_DP = 1024
SLAB = 2048
PAIRS = 4096
NEGS = 16384
CORPUS = 32768
N_DP = 16


def draw_queries(key, part):
    key_base, key_scale, key_pick, key_boost = jax.random.split(key, 4)
    row_scale = jnp.exp(jax.random.uniform(key_scale, (PAIRS, 1), jnp.float32, math.log(0.5), math.log(5.0)))
    chosen = jax.random.randint(key_pick, (PAIRS, 1), 0, 16) == 0
    boost = jax.random.uniform(key_boost, (PAIRS, 1), jnp.float32, 40.0, 62.0)
    base_values = jnp.clip(jax.random.normal(key_base, (PAIRS, E), jnp.float32), -4.0, 4.0)
    drawn = base_values * row_scale
    strong = jnp.clip(base_values, -1.7, 1.7) * boost
    return jnp.where(chosen, strong, drawn).astype(jnp.bfloat16)


def set_ends(drawn, own_key, least, largest):
    longest = drawn.shape.index(max(drawn.shape))
    spots = []
    for shift in (0, 1):
        where = [jax.random.randint(jax.random.fold_in(own_key, axis), (), 0, length) for axis, length in enumerate(drawn.shape)]
        where[longest] = (where[longest] + shift) % drawn.shape[longest]
        spots.append(tuple(where))
    return drawn.at[spots[0]].set(least).at[spots[1]].set(largest)


def block_levels(key, extent, pieces, least, high):
    factor_of = 1.0
    for axis_at, parts in pieces:
        steps = jax.random.uniform(jax.random.fold_in(jax.random.fold_in(key, 6), axis_at), (parts,), jnp.float32, least / len(pieces), high / len(pieces))
        factor_of = factor_of * jnp.repeat(jnp.exp(steps), extent[axis_at] // parts).reshape((-1,) + (1,) * (len(extent) - 1 - axis_at))
    return factor_of


def scatter_about(own_key, shape, width, reach, pieces=(), held_as=jnp.bfloat16):
    values = jax.random.normal(own_key, shape, jnp.float32) * width
    if len(pieces) > 0:
        values = block_levels(own_key, shape, pieces, -0.22, 0.18) * values
    return jnp.clip(values, min=-reach, max=reach).astype(held_as)


def setup_inputs(seed: int = 0) -> dict:
    splits = jax.random.split(jax.random.key(seed), 8)
    return {
        "queries": draw_queries(jax.random.fold_in(splits[7], 71), 0),
        "item_features": scatter_about(splits[1], (PAIRS, F), 1.0, 6.0, ((0, 16), (1, 2))),
        "corpus": scatter_about(splits[2], (CORPUS, F), 1.0, 6.0, ((0, 16), (1, 2))),
        "sample_ids": set_ends(jax.random.randint(splits[3], (NEGS,), 0, SLAB), jax.random.fold_in(splits[3], 1), 0, SLAB - 1).astype(jnp.int32),
        "sample_shift": jnp.clip(jax.random.uniform(splits[4], (NEGS,), jnp.float32, -2.0, 2.0) * block_levels(splits[4], (NEGS,), ((0, 16),), -0.4, 0.0), -2.0, 2.0).astype(jnp.bfloat16),
        "w1": scatter_about(splits[5], (F, H), F ** -0.5, 0.125, ((1, 2),)),
        "w2": scatter_about(splits[6], (H, E), H ** -0.5, 0.1875, ((0, 2),)),
    }


def reference(queries, item_features, corpus, sample_ids, sample_shift, w1, w2):
    score_scale = E ** (-0.5)
    owner_rows = jnp.arange(NEGS, dtype=jnp.int32) // NEG_DP
    picked = jnp.take(corpus, owner_rows * SLAB + sample_ids.astype(jnp.int32), axis=0)
    features = jnp.concatenate([item_features, picked], 0)
    pre_act = jnp.dot(features, w1, preferred_element_type=jnp.float32)
    hidden = jnp.maximum(pre_act, 0.0).astype(jnp.bfloat16)
    embedded = jnp.dot(hidden, w2, preferred_element_type=jnp.float32)
    inverse = lax.rsqrt(lax.optimization_barrier(jnp.mean(embedded * embedded, -1, keepdims=True)) + 1e-06)
    normed = (embedded * inverse).astype(jnp.bfloat16)
    bias_wide = jnp.concatenate([jnp.zeros((PAIRS,), jnp.float32), -sample_shift.astype(jnp.float32)])
    query_blocks = queries.reshape(N_DP, Q_DP, E)
    positive_blocks = normed[:PAIRS].reshape(N_DP, Q_DP, E)

    def one_block(grad_acc, inputs):
        query_blk, positive_blk = inputs
        logits = score_scale * jnp.dot(query_blk, normed.T, preferred_element_type=jnp.float32) + bias_wide
        highest = lax.optimization_barrier(jnp.max(logits, -1, keepdims=True))
        row_sum = lax.optimization_barrier(jnp.sum(jnp.exp(logits - highest), -1, keepdims=True))
        log_total = highest + jnp.log(row_sum)
        positive = score_scale * lax.optimization_barrier(jnp.sum(query_blk.astype(jnp.float32) * positive_blk.astype(jnp.float32), -1))
        loss_blk = log_total[:, 0] - positive
        softmax = jnp.exp(logits - log_total).astype(jnp.bfloat16)
        grad_blk = score_scale * (jnp.dot(softmax, normed, preferred_element_type=jnp.float32) - positive_blk.astype(jnp.float32))
        grad_acc = grad_acc + jnp.dot(softmax.T, query_blk, preferred_element_type=jnp.float32)
        return (grad_acc, (loss_blk, grad_blk))
    grad_acc, outputs = lax.scan(one_block, jnp.zeros((PAIRS + NEGS, E), jnp.float32), (query_blocks, positive_blocks))
    loss_blocks, grad_blocks = outputs
    target = jnp.concatenate([queries.astype(jnp.float32), jnp.zeros((NEGS, E), jnp.float32)], 0)
    grad_normed = score_scale * (grad_acc - target)
    grad_embed = inverse * grad_normed - inverse ** 3 * embedded * lax.optimization_barrier(jnp.sum(grad_normed * embedded, -1, keepdims=True)) / E
    grad_back = grad_embed.astype(jnp.bfloat16)
    grad_pre = jnp.where(pre_act > 0, jnp.dot(grad_back, w2.T, preferred_element_type=jnp.float32), 0.0).astype(jnp.bfloat16)
    grad_w2 = jnp.dot(hidden.T, grad_back, preferred_element_type=jnp.float32)
    grad_w1 = jnp.dot(features.T, grad_pre, preferred_element_type=jnp.float32)
    return (loss_blocks.reshape(PAIRS), grad_blocks.reshape(PAIRS, E), grad_w1, grad_w2)
```

```python
import jax
import jax.numpy as jnp
from jax import lax
from jax.sharding import PartitionSpec as P

F32 = jnp.float32
BF16 = jnp.bfloat16
LANES = 128


def mm(a, b):
    return jnp.dot(a, b, preferred_element_type=F32)


def pack(x):
    return jnp.concatenate([x[:, i : i + LANES] for i in range(0, x.shape[1], LANES)], 0)


def unpack(x, rows, cols):
    x = x.reshape(x.shape[0], cols // LANES, rows, LANES)
    return jnp.concatenate([x[:, i].reshape(-1, LANES) for i in range(cols // LANES)], 1)


def per_device(queries, item_features, corpus, sample_ids, sample_shift, w1, w2):
    groups = lax.axis_size("group")
    member = lax.axis_index("group")
    n_dp = lax.axis_size("dp")
    d = lax.axis_index("dp")
    query_rows, emb = queries.shape
    quota = query_rows // groups
    negs = sample_ids.shape[0] // groups
    rows = quota + negs
    fg = item_features.shape[1]
    scale = emb ** (-0.5)

    def shift(x, s):
        return lax.ppermute(x, "group", [(i, (i + s) % groups) for i in range(groups)])

    def at(x, i):
        return lax.dynamic_index_in_dim(x, lax.rem(i, groups), 0, keepdims=False)

    w1_rows, w2_rows = w1.shape[0] // n_dp, w2.shape[0] // n_dp
    w1_piece = pack(lax.dynamic_slice_in_dim(w1, d * w1_rows, w1_rows))
    w2_piece = pack(lax.dynamic_slice_in_dim(w2, d * w2_rows, w2_rows))
    piece = jnp.concatenate([w1_piece, w2_piece], 0)
    pieces = [pack(queries)] + [shift(piece, s) for s in range(1, groups)]
    shared = lax.all_gather(jnp.concatenate(pieces, 0), "dp", axis=0, tiled=False)
    nq, n1, n2 = pieces[0].shape[0], w1_piece.shape[0], w2_piece.shape[0]
    q_all = unpack(shared[:, :nq], query_rows, emb)
    w1s, w2s = [w1], [w2]
    for s in range(1, groups):
        at0 = nq + (s - 1) * (n1 + n2)
        w1s.append(unpack(shared[:, at0 : at0 + n1], w1_rows, w1.shape[1]))
        w2s.append(unpack(shared[:, at0 + n1 : at0 + n1 + n2], w2_rows, emb))

    picked = corpus.at[sample_ids].get(mode="promise_in_bounds")
    local = jnp.concatenate(
        [item_features.reshape(groups, quota, fg), picked.reshape(groups, negs, fg)], 1
    )
    mine = [at(local, member)] + [shift(at(local, member + s), s) for s in range(1, groups)]
    feats = jnp.zeros((rows, groups * fg), BF16)
    for s in range(groups):
        feats = lax.dynamic_update_slice_in_dim(
            feats, mine[s], lax.rem(member + groups - s, groups) * fg, 1
        )
    local, feats = lax.optimization_barrier((local, feats))
    rest_rows = (groups - 1) * rows
    rest = jnp.zeros((rest_rows, groups * fg), BF16)
    for s in range(groups):
        blocks = jnp.concatenate([at(local, member + s + t) for t in range(1, groups)], 0)
        if s > 0:
            blocks = shift(blocks, s)
        rest = lax.dynamic_update_slice_in_dim(
            rest, blocks, lax.rem(member + groups - s, groups) * fg, 1
        )

    embedded = jnp.zeros((rows, emb), F32)
    pre_own = None
    for s in range(groups):
        pre = mm(feats, w1s[s])
        hid = jnp.maximum(pre, 0.0).astype(BF16)
        if s == 0:
            pre_own, hid_own = pre, hid
        embedded = embedded + mm(hid, w2s[s])
    inverse = lax.rsqrt(jnp.mean(embedded * embedded, -1, keepdims=True) + 1e-06)
    normed = (embedded * inverse).astype(BF16)
    shift_own = lax.dynamic_slice_in_dim(sample_shift, member * negs, negs).astype(F32)
    bias = jnp.concatenate([jnp.zeros((quota,), F32), -shift_own])

    logits = scale * lax.dot_general(
        q_all, normed, (((1,), (1,)), ((), ())), preferred_element_type=F32
    ) + bias
    axes = ("dp", "group")
    top = jnp.max(logits, -1)
    row_sum = jnp.sum(jnp.exp(logits - top[:, None]), -1)
    largest = lax.pmax(top, axes)
    row_sum = lax.psum(row_sum * jnp.exp(top - largest), axes)
    log_total = largest + jnp.log(row_sum)
    softmax = jnp.exp(logits - log_total[:, None]).astype(BF16)

    query_own = lax.dynamic_slice_in_dim(queries, member * quota, quota).astype(F32)
    positive_own = normed[:quota].astype(F32)
    positive = scale * jnp.sum(query_own * positive_own, -1)
    query_loss = (
        lax.dynamic_slice_in_dim(log_total, d * query_rows + member * quota, quota) - positive
    )
    grad_hat = lax.dot_general(
        softmax, q_all, (((0,), (0,)), ((), ())), preferred_element_type=F32
    )
    query_part = mm(softmax, normed)
    query_sum = lax.psum_scatter(query_part, axes, scatter_dimension=0, tiled=True)
    grad_query = scale * (query_sum - positive_own)

    target = jnp.concatenate([query_own, jnp.zeros((negs, emb), F32)], 0)
    grad_normed = scale * (grad_hat - target)
    along = jnp.sum(grad_normed * embedded, -1, keepdims=True)
    grad_embed = (
        inverse * grad_normed - inverse**3 * embedded * along / emb
    ).astype(BF16)

    pre_rest = mm(rest, w1)
    hid_rest = jnp.maximum(pre_rest, 0.0).astype(BF16)
    back = jnp.concatenate(
        [grad_embed] + [shift(grad_embed, (groups - t) % groups) for t in range(1, groups)], 0
    )
    mask = jnp.concatenate([pre_own, pre_rest], 0) > 0
    grad_pre = jnp.where(mask, mm(back, w2.T), 0.0).astype(BF16)
    hid_all = jnp.concatenate([hid_own, hid_rest], 0)
    over_rows = (((0,), (0,)), ((), ()))
    grad_w2 = lax.dot_general(hid_all, back, over_rows, preferred_element_type=F32)
    feats_all = jnp.concatenate([feats, rest], 0)
    grad_w1 = lax.dot_general(feats_all, grad_pre, over_rows, preferred_element_type=F32)
    grad_w1, grad_w2 = lax.psum((grad_w1, grad_w2), "dp")
    return (query_loss, grad_query, grad_w1, grad_w2)


def solution(mesh):
    in_specs = (
        P("dp", None),
        P("dp", "group"),
        P("dp", "group"),
        P("dp"),
        P("dp"),
        P(None, "group"),
        P("group", None),
    )
    out_specs = (P(("dp", "group")), P(("dp", "group"), None), P(None, "group"), P("group", None))
    return jax.shard_map(
        per_device, mesh=mesh, in_specs=in_specs, out_specs=out_specs, check_vma=False
    )
```

```python
import functools

import jax
import jax.numpy as jnp
from jax import lax
from jax.experimental import pallas as pl
from jax.experimental.pallas import tpu as pltpu
from jax.sharding import PartitionSpec as P

F32 = jnp.float32
BF16 = jnp.bfloat16
LANES = 128
MESH = pl.DeviceIdType.MESH
ANY = pl.BlockSpec(memory_space=pl.ANY)
VMEM = pl.BlockSpec(memory_space=pltpu.VMEM)


def bits_of(n):
    return [1 << i for i in range(n.bit_length() - 1)]


def partner(axis, step):
    i = lax.axis_index(axis)
    bit = lax.rem(lax.div(i, step), 2)
    return bit, {axis: i + step - 2 * step * bit}


def greet(peers):
    barrier = pltpu.get_barrier_semaphore()
    for peer in peers:
        pl.semaphore_signal(barrier, inc=1, device_id=peer, device_id_type=MESH)
    pl.semaphore_wait(barrier, len(peers))


def score_kernel(groups, n_dp, local, queries, normed, normed_t, bias,
                 total_ref, hat_ref, part_ref, rest_ref,
                 logits, stats, arrived, send_sem, recv_sem, fsend, frecv):
    tiles, cols, width = logits.shape
    emb = normed.shape[1]
    scale = emb ** (-0.5)
    member = lax.axis_index("group")
    rounds = [("dp", b) for b in bits_of(n_dp)] + [("group", b) for b in bits_of(groups)]
    peers = [partner(a, b)[1] for a, b in rounds]
    others = [lax.rem(member + s, groups) for s in range(1, groups)]
    extra = [{"group": o} for o in others] if groups > 2 else []
    greet(peers + extra)
    copies = []
    for s in range(1, groups):
        for t in range(1, groups):
            k = (s - 1) * (groups - 1) + t - 1
            copy = pltpu.make_async_remote_copy(
                src_ref=local.at[lax.rem(member + s + t, groups)],
                dst_ref=rest_ref.at[s - 1, t - 1],
                send_sem=fsend.at[k], recv_sem=frecv.at[k],
                device_id={"group": others[s - 1]}, device_id_type=MESH)
            copy.start()
            copies.append(copy)

    def first(i, carry):
        q = queries[pl.ds(pl.multiple_of(i * width, width), width), :]
        block = scale * lax.dot_general(
            normed[...], q, (((1,), (1,)), ((), ())), preferred_element_type=F32) + bias[...]
        logits[i] = block
        top = jnp.max(block, 0, keepdims=True)
        stats[0, 0, pl.ds(i, 1), :] = top
        stats[0, 1, pl.ds(i, 1), :] = jnp.sum(jnp.exp(block - top), 0, keepdims=True)
        return carry

    lax.fori_loop(0, tiles, first, 0)
    for r, peer in enumerate(peers):
        copy = pltpu.make_async_remote_copy(
            src_ref=stats.at[r], dst_ref=arrived.at[r],
            send_sem=send_sem.at[r], recv_sem=recv_sem.at[r],
            device_id=peer, device_id_type=MESH)
        copy.start()
        copy.wait()
        m0, s0, m1, s1 = stats[r, 0], stats[r, 1], arrived[r, 0], arrived[r, 1]
        top = jnp.maximum(m0, m1)
        stats[r + 1, 0] = top
        stats[r + 1, 1] = s0 * jnp.exp(m0 - top) + s1 * jnp.exp(m1 - top)
    last = len(peers)
    total_ref[...] = stats[last, 0] + jnp.log(stats[last, 1])
    hat_ref[...] = jnp.zeros_like(hat_ref)

    def second(i, carry):
        at_i = pl.ds(pl.multiple_of(i * width, width), width)
        p = jnp.exp(logits[i] - total_ref[pl.ds(i, 1), :]).astype(BF16)
        hat_ref[...] += mm(p, queries[at_i, :])
        part_ref[at_i, :] = mm(normed_t[...], p).T
        return carry

    lax.fori_loop(0, tiles, second, 0)
    for copy in copies:
        copy.wait()


def score(groups, n_dp, local, queries, normed, bias):
    rows, fg = local.shape[1:]
    width = 256
    total, emb = queries.shape
    tiles = total // width
    rounds = len(bits_of(n_dp)) + len(bits_of(groups))
    n_copies = (groups - 1) ** 2
    return pl.pallas_call(
        functools.partial(score_kernel, groups, n_dp),
        out_shape=(
            jax.ShapeDtypeStruct((tiles, width), F32),
            jax.ShapeDtypeStruct((rows, emb), F32),
            jax.ShapeDtypeStruct((total, emb), F32),
            jax.ShapeDtypeStruct((groups - 1, groups - 1, rows, fg), BF16),
        ),
        in_specs=[ANY, VMEM, VMEM, VMEM, VMEM],
        out_specs=(VMEM, VMEM, VMEM, ANY),
        scratch_shapes=[
            pltpu.VMEM((tiles, rows, width), F32),
            pltpu.VMEM((rounds + 1, 2, tiles, width), F32),
            pltpu.VMEM((rounds, 2, tiles, width), F32),
            pltpu.SemaphoreType.DMA((rounds,)),
            pltpu.SemaphoreType.DMA((rounds,)),
            pltpu.SemaphoreType.DMA((n_copies,)),
            pltpu.SemaphoreType.DMA((n_copies,)),
        ],
        compiler_params=pltpu.CompilerParams(
            collective_id=0, has_side_effects=True, vmem_limit_bytes=44 << 20),
        name="score",
    )(local, queries, normed, normed.T, bias)


def reduce_kernel(plans, n_peers_of, *refs):
    n = len(plans)
    ins, outs = refs[:n], refs[n : 2 * n]
    accs, sends, recvs = (refs[2 * n + i * n : 3 * n + i * n] for i in range(3))
    send_sem, recv_sem, gsend, grecv = refs[5 * n :]
    greet([partner(a, b)[1] for a, b in n_peers_of])
    live = {}

    def begin(i, r):
        rounds, bases, _ = plans[i]
        bit, peer = partner(*rounds[r])
        half = ins[i].shape[0] >> (r + 1)
        at0 = ins[i].shape[0] - 2 * half

        def stage(j, carry):
            if r == 0:
                block = ins[i][bases(j) + (1 - bit) * bases(half)]
            else:
                block = accs[i][(1 - bit) * half + j]
            sends[i][at0 + j] = block.astype(BF16)
            return carry

        lax.fori_loop(0, half, stage, 0)
        copy = pltpu.make_async_remote_copy(
            src_ref=sends[i].at[pl.ds(at0, half)], dst_ref=recvs[i].at[pl.ds(at0, half)],
            send_sem=send_sem.at[i, r], recv_sem=recv_sem.at[i, r],
            device_id=peer, device_id_type=MESH)
        copy.start()
        live[i] = copy

    def finish(i, r):
        rounds, bases, _ = plans[i]
        bit, _ = partner(*rounds[r])
        half = ins[i].shape[0] >> (r + 1)
        at0 = ins[i].shape[0] - 2 * half
        live[i].wait()

        def add(j, carry):
            if r == 0:
                block = ins[i][bases(j) + bit * bases(half)]
            else:
                block = accs[i][bit * half + j]
            accs[i][j] = block + recvs[i][at0 + j].astype(F32)
            return carry

        lax.fori_loop(0, half, add, 0)

    def place(i, r):
        rounds = plans[i][0]
        return sum(partner(*rounds[k])[0] * (ins[i].shape[0] >> (k + 1)) for k in range(r + 1))

    def share(i, r):
        peer = partner(*plans[i][0][r])[1]
        span = pl.ds(place(i, r), ins[i].shape[0] >> (r + 1))
        copy = pltpu.make_async_remote_copy(
            src_ref=outs[i].at[span], dst_ref=outs[i].at[span],
            send_sem=gsend.at[i, r], recv_sem=grecv.at[i, r],
            device_id=peer, device_id_type=MESH)
        copy.start()
        live[i] = copy

    def advance(i, step):
        rounds, _, gather = plans[i]
        k = len(rounds)
        if 0 < step <= k:
            finish(i, step - 1)
        if step < k:
            begin(i, step)
        elif step == k and not gather:
            outs[i][0] = accs[i][0]
        elif gather and step <= 2 * k:
            if step == k:
                outs[i][place(i, k - 1)] = accs[i][0].astype(BF16)
            else:
                live[i].wait()
            if step < 2 * k:
                share(i, 2 * k - 1 - step)

    steps = max(len(p[0]) * (2 if p[2] else 1) for p in plans) + 1
    for step in range(steps):
        for i in range(n):
            advance(i, step)


def bit_place(steps, j):
    k = len(steps)
    out = 0
    for i, step in enumerate(steps):
        weight = 1 << (k - 1 - i)
        if isinstance(j, int):
            out += (j // weight) % 2 * step
        else:
            out = out + lax.rem(lax.div(j, weight), 2) * step
    return out


def reduce_all(groups, n_dp, arrays):
    plans = []
    for x, rounds, gather in arrays:
        n = x.shape[0]
        if gather:
            steps = [n >> (k + 1) for k in range(len(rounds))]
        else:
            steps = [b * groups if a == "dp" else b for a, b in rounds]
        plans.append((rounds, functools.partial(bit_place, steps), gather))
    xs = [x for x, _, _ in arrays]
    most = max(len(p[0]) for p in plans)
    peers = [("dp", b) for b in bits_of(n_dp)] + [("group", b) for b in bits_of(groups)]
    sems = pltpu.SemaphoreType.DMA((len(xs), most))
    return pl.pallas_call(
        functools.partial(reduce_kernel, plans, peers),
        out_shape=tuple(
            jax.ShapeDtypeStruct(x.shape, BF16) if g else jax.ShapeDtypeStruct((1,) + x.shape[1:], F32)
            for x, _, g in arrays),
        in_specs=[VMEM] * len(xs),
        out_specs=(VMEM,) * len(xs),
        scratch_shapes=[pltpu.VMEM((x.shape[0] // 2,) + x.shape[1:], F32) for x in xs]
        + [pltpu.VMEM(x.shape, BF16) for x in xs] * 2 + [sems] * 4,
        compiler_params=pltpu.CompilerParams(
            collective_id=1, has_side_effects=True, vmem_limit_bytes=48 << 20),
        name="reduce_all",
    )(*xs)


def mm(a, b):
    return jnp.dot(a, b, preferred_element_type=F32)


def pack(x):
    return jnp.concatenate([x[:, i : i + LANES] for i in range(0, x.shape[1], LANES)], 0)


def unpack(x, rows, cols):
    x = x.reshape(x.shape[0], cols // LANES, rows, LANES)
    return jnp.concatenate([x[:, i].reshape(-1, LANES) for i in range(cols // LANES)], 1)


def per_device(queries, item_features, corpus, sample_ids, sample_shift, w1, w2):
    groups = lax.axis_size("group")
    member = lax.axis_index("group")
    n_dp = lax.axis_size("dp")
    d = lax.axis_index("dp")
    query_rows, emb = queries.shape
    quota = query_rows // groups
    negs = sample_ids.shape[0] // groups
    rows = quota + negs
    fg = item_features.shape[1]
    scale = emb ** (-0.5)

    def shift(x, s):
        return lax.ppermute(x, "group", [(i, (i + s) % groups) for i in range(groups)])

    def at(x, i):
        return lax.dynamic_index_in_dim(x, lax.rem(i, groups), 0, keepdims=False)

    w1_rows, w2_rows = w1.shape[0] // n_dp, w2.shape[0] // n_dp
    w1_piece = pack(lax.dynamic_slice_in_dim(w1, d * w1_rows, w1_rows))
    w2_piece = pack(lax.dynamic_slice_in_dim(w2, d * w2_rows, w2_rows))
    piece = jnp.concatenate([w1_piece, w2_piece], 0)
    pieces = [pack(queries)] + [shift(piece, s) for s in range(1, groups)]
    shared = lax.all_gather(jnp.concatenate(pieces, 0), "dp", axis=0, tiled=False)
    nq, n1, n2 = pieces[0].shape[0], w1_piece.shape[0], w2_piece.shape[0]
    q_all = unpack(shared[:, :nq], query_rows, emb)
    w1s, w2s = [w1], [w2]
    for s in range(1, groups):
        at0 = nq + (s - 1) * (n1 + n2)
        w1s.append(unpack(shared[:, at0 : at0 + n1], w1_rows, w1.shape[1]))
        w2s.append(unpack(shared[:, at0 + n1 : at0 + n1 + n2], w2_rows, emb))

    picked = corpus.at[sample_ids].get(mode="promise_in_bounds")
    local = jnp.concatenate(
        [item_features.reshape(groups, quota, fg), picked.reshape(groups, negs, fg)], 1
    )
    mine = [at(local, member)] + [shift(at(local, member + s), s) for s in range(1, groups)]
    feats = jnp.zeros((rows, groups * fg), BF16)
    for s in range(groups):
        feats = lax.dynamic_update_slice_in_dim(
            feats, mine[s], lax.rem(member + groups - s, groups) * fg, 1
        )
    embedded = jnp.zeros((rows, emb), F32)
    pre_own = None
    for s in range(groups):
        pre = mm(feats, w1s[s])
        hid = jnp.maximum(pre, 0.0).astype(BF16)
        if s == 0:
            pre_own, hid_own = pre, hid
        embedded = embedded + mm(hid, w2s[s])
    inverse = lax.rsqrt(jnp.mean(embedded * embedded, -1, keepdims=True) + 1e-06)
    normed = (embedded * inverse).astype(BF16)
    shift_own = lax.dynamic_slice_in_dim(sample_shift, member * negs, negs).astype(F32)
    bias = jnp.concatenate([jnp.zeros((quota,), F32), -shift_own])

    log_total, grad_hat, query_part, landed = score(
        groups, n_dp, local, q_all, normed, bias[:, None])
    log_total = log_total.reshape(-1)
    rest = jnp.zeros(((groups - 1) * rows, groups * fg), BF16)
    for s in range(groups):
        if s > 0:
            blocks = landed[s - 1].reshape(-1, fg)
        else:
            blocks = jnp.concatenate([at(local, member + t) for t in range(1, groups)], 0)
        rest = lax.dynamic_update_slice_in_dim(
            rest, blocks, lax.rem(member + groups - s, groups) * fg, 1
        )

    query_own = lax.dynamic_slice_in_dim(queries, member * quota, quota).astype(F32)
    positive_own = normed[:quota].astype(F32)
    positive = scale * jnp.sum(query_own * positive_own, -1)
    query_loss = (
        lax.dynamic_slice_in_dim(log_total, d * query_rows + member * quota, quota) - positive
    )
    target = jnp.concatenate([query_own, jnp.zeros((negs, emb), F32)], 0)
    grad_normed = scale * (grad_hat - target)
    along = jnp.sum(grad_normed * embedded, -1, keepdims=True)
    grad_embed = (
        inverse * grad_normed - inverse**3 * embedded * along / emb
    ).astype(BF16)

    pre_rest = mm(rest, w1)
    hid_rest = jnp.maximum(pre_rest, 0.0).astype(BF16)
    back = jnp.concatenate(
        [grad_embed] + [shift(grad_embed, (groups - t) % groups) for t in range(1, groups)], 0
    )
    mask = jnp.concatenate([pre_own, pre_rest], 0) > 0
    grad_pre = jnp.where(mask, mm(back, w2.T), 0.0).astype(BF16)
    hid_all = jnp.concatenate([hid_own, hid_rest], 0)
    over_rows = (((0,), (0,)), ((), ()))
    grad_w2 = lax.dot_general(hid_all, back, over_rows, preferred_element_type=F32)
    feats_all = jnp.concatenate([feats, rest], 0)
    grad_w1 = lax.dot_general(feats_all, grad_pre, over_rows, preferred_element_type=F32)
    dp_bits = bits_of(n_dp)
    near, far = dp_bits[:1], dp_bits[:1:-1]
    along_first = [("dp", b) for b in near + dp_bits[1:2] + far]
    along_last = [("dp", b) for b in near + far + dp_bits[1:2]]
    query_order = (
        [("dp", near[0])]
        + [("group", b) for b in bits_of(groups)]
        + [("dp", b) for b in dp_bits[1:2] + far]
    )
    pad = -grad_w2.shape[0] % (16 * n_dp)
    padded = jnp.pad(grad_w2, ((0, pad), (0, 0)))
    halves = grad_w1.reshape(2, n_dp, -1, grad_w1.shape[1])
    out_a, out_b, out_w2, query_sum = reduce_all(groups, n_dp, [
        (halves[0], along_last, True),
        (halves[1], along_first, True),
        (padded.reshape(n_dp, -1, emb), along_first, True),
        (query_part.reshape(n_dp * groups, quota, emb), query_order, False),
    ])
    grad_query = scale * (query_sum[0] - positive_own)
    grad_w1 = jnp.concatenate([out_a, out_b], 0).reshape(grad_w1.shape).astype(F32)
    grad_w2 = out_w2.reshape(padded.shape)[: grad_w2.shape[0]].astype(F32)
    return (query_loss, grad_query, grad_w1, grad_w2)


def solution(mesh):
    in_specs = (
        P("dp", None),
        P("dp", "group"),
        P("dp", "group"),
        P("dp"),
        P("dp"),
        P(None, "group"),
        P("group", None),
    )
    out_specs = (P(("dp", "group")), P(("dp", "group"), None), P(None, "group"), P("group", None))
    return jax.shard_map(
        per_device, mesh=mesh, in_specs=in_specs, out_specs=out_specs, check_vma=False
    )
```

```python
import functools

import jax
import jax.numpy as jnp
from jax import lax
from jax.experimental import pallas as pl
from jax.experimental.pallas import tpu as pltpu
from jax.sharding import PartitionSpec as P

F32 = jnp.float32
BF16 = jnp.bfloat16
MESH = pl.DeviceIdType.MESH
ANY = pl.BlockSpec(memory_space=pl.ANY)
VMEM = pl.BlockSpec(memory_space=pltpu.VMEM)


def mm(a, b):
    return jnp.dot(a, b, preferred_element_type=F32)


def bits_of(n):
    return [1 << i for i in range(n.bit_length() - 1)]


def partner(axis, step):
    i = lax.axis_index(axis)
    bit = lax.rem(lax.div(i, step), 2)
    return bit, {axis: i + step - 2 * step * bit}


def greet(peers):
    barrier = pltpu.get_barrier_semaphore()
    for peer in peers:
        pl.semaphore_signal(barrier, inc=1, device_id=peer, device_id_type=MESH)
    pl.semaphore_wait(barrier, len(peers))


def score_kernel(groups, n_dp, local, queries, normed, normed_t, bias,
                 total_ref, hat_ref, part_ref, rest_ref,
                 logits, stats, arrived, send_sem, recv_sem, fsend, frecv):
    tiles, cols, width = logits.shape
    emb = normed.shape[1]
    scale = emb ** (-0.5)
    member = lax.axis_index("group")
    rounds = [("dp", b) for b in bits_of(n_dp)] + [("group", b) for b in bits_of(groups)]
    peers = [partner(a, b)[1] for a, b in rounds]
    others = [lax.rem(member + s, groups) for s in range(1, groups)]
    extra = [{"group": o} for o in others] if groups > 2 else []
    greet(peers + extra)
    copies = []
    for s in range(1, groups):
        for t in range(1, groups):
            k = (s - 1) * (groups - 1) + t - 1
            copy = pltpu.make_async_remote_copy(
                src_ref=local.at[(s + t) % groups],
                dst_ref=rest_ref.at[s - 1, t - 1],
                send_sem=fsend.at[k], recv_sem=frecv.at[k],
                device_id={"group": others[s - 1]}, device_id_type=MESH)
            copy.start()
            copies.append(copy)

    def first(i, carry):
        q = queries[pl.ds(pl.multiple_of(i * width, width), width), :]
        block = scale * lax.dot_general(
            normed[...], q, (((1,), (1,)), ((), ())), preferred_element_type=F32) + bias[...]
        logits[i] = block
        top = jnp.max(block, 0, keepdims=True)
        stats[0, 0, pl.ds(i, 1), :] = top
        stats[0, 1, pl.ds(i, 1), :] = jnp.sum(jnp.exp(block - top), 0, keepdims=True)
        return carry

    lax.fori_loop(0, tiles, first, 0)
    for r, peer in enumerate(peers):
        copy = pltpu.make_async_remote_copy(
            src_ref=stats.at[r], dst_ref=arrived.at[r],
            send_sem=send_sem.at[r], recv_sem=recv_sem.at[r],
            device_id=peer, device_id_type=MESH)
        copy.start()
        copy.wait()
        m0, s0, m1, s1 = stats[r, 0], stats[r, 1], arrived[r, 0], arrived[r, 1]
        top = jnp.maximum(m0, m1)
        stats[r + 1, 0] = top
        stats[r + 1, 1] = s0 * jnp.exp(m0 - top) + s1 * jnp.exp(m1 - top)
    last = len(peers)
    total_ref[...] = stats[last, 0] + jnp.log(stats[last, 1])
    hat_ref[...] = jnp.zeros_like(hat_ref)

    def second(i, carry):
        at_i = pl.ds(pl.multiple_of(i * width, width), width)
        p = jnp.exp(logits[i] - total_ref[pl.ds(i, 1), :]).astype(BF16)
        hat_ref[...] += mm(p, queries[at_i, :])
        part_ref[at_i, :] = mm(normed_t[...], p).T
        return carry

    lax.fori_loop(0, tiles, second, 0)
    for copy in copies:
        copy.wait()


def score(groups, n_dp, local, queries, normed, bias):
    rows, fg = local.shape[1:]
    width = 256
    total, emb = queries.shape
    tiles = total // width
    rounds = len(bits_of(n_dp)) + len(bits_of(groups))
    n_copies = (groups - 1) ** 2
    return pl.pallas_call(
        functools.partial(score_kernel, groups, n_dp),
        out_shape=(
            jax.ShapeDtypeStruct((tiles, width), F32),
            jax.ShapeDtypeStruct((rows, emb), F32),
            jax.ShapeDtypeStruct((total, emb), F32),
            jax.ShapeDtypeStruct((groups - 1, groups - 1, rows, fg), BF16),
        ),
        in_specs=[ANY, VMEM, VMEM, VMEM, VMEM],
        out_specs=(VMEM, VMEM, VMEM, ANY),
        scratch_shapes=[
            pltpu.VMEM((tiles, rows, width), F32),
            pltpu.VMEM((rounds + 1, 2, tiles, width), F32),
            pltpu.VMEM((rounds, 2, tiles, width), F32),
            pltpu.SemaphoreType.DMA((rounds,)),
            pltpu.SemaphoreType.DMA((rounds,)),
            pltpu.SemaphoreType.DMA((n_copies,)),
            pltpu.SemaphoreType.DMA((n_copies,)),
        ],
        compiler_params=pltpu.CompilerParams(
            collective_id=0, has_side_effects=True, vmem_limit_bytes=44 << 20),
        name="score",
    )(local, queries, normed, normed.T, bias)


def reduce_kernel(plans, n_in, n_peers_of, *refs):
    n = len(plans)
    ins, refs = refs[:n_in], refs[n_in:]
    outs = refs[:n]
    accs, sends, recvs = (refs[n + i * n : 2 * n + i * n] for i in range(3))
    send_sem, recv_sem, gsend, grecv = refs[4 * n :]
    greet([partner(a, b)[1] for a, b in n_peers_of])
    live = {}

    def begin(i, r):
        rounds, bases, _, source, start, count = plans[i]
        bit, peer = partner(*rounds[r])
        half = count >> (r + 1)
        at0 = count - 2 * half

        def stage(j, carry):
            if r == 0:
                block = ins[source][start + bases(j) + (1 - bit) * bases(half)]
            else:
                block = accs[i][(1 - bit) * half + j]
            sends[i][at0 + j] = block.astype(BF16)
            return carry

        lax.fori_loop(0, half, stage, 0)
        copy = pltpu.make_async_remote_copy(
            src_ref=sends[i].at[pl.ds(at0, half)], dst_ref=recvs[i].at[pl.ds(at0, half)],
            send_sem=send_sem.at[i, r], recv_sem=recv_sem.at[i, r],
            device_id=peer, device_id_type=MESH)
        copy.start()
        live[i] = copy

    def finish(i, r):
        rounds, bases, _, source, start, count = plans[i]
        bit, _ = partner(*rounds[r])
        half = count >> (r + 1)
        at0 = count - 2 * half
        live[i].wait()

        def add(j, carry):
            if r == 0:
                block = ins[source][start + bases(j) + bit * bases(half)]
            else:
                block = accs[i][bit * half + j]
            accs[i][j] = block + recvs[i][at0 + j].astype(F32)
            return carry

        lax.fori_loop(0, half, add, 0)

    def place(i, r):
        rounds = plans[i][0]
        return sum(partner(*rounds[k])[0] * (plans[i][5] >> (k + 1)) for k in range(r + 1))

    def share(i, r):
        peer = partner(*plans[i][0][r])[1]
        span = pl.ds(place(i, r), plans[i][5] >> (r + 1))
        copy = pltpu.make_async_remote_copy(
            src_ref=outs[i].at[span], dst_ref=outs[i].at[span],
            send_sem=gsend.at[i, r], recv_sem=grecv.at[i, r],
            device_id=peer, device_id_type=MESH)
        copy.start()
        live[i] = copy

    def advance(i, step):
        rounds, _, gather = plans[i][:3]
        k = len(rounds)
        if 0 < step <= k:
            finish(i, step - 1)
        if step < k:
            begin(i, step)
        elif step == k and not gather:
            outs[i][0] = accs[i][0]
        elif gather and step <= 2 * k:
            if step == k:
                outs[i][place(i, k - 1)] = accs[i][0].astype(BF16)
            else:
                live[i].wait()
            if step < 2 * k:
                share(i, 2 * k - 1 - step)

    steps = max(len(p[0]) * (2 if p[2] else 1) for p in plans) + 1
    for step in range(steps):
        for i in range(n):
            advance(i, step)


def bit_place(steps, j):
    k = len(steps)
    out = 0
    for i, step in enumerate(steps):
        weight = 1 << (k - 1 - i)
        if isinstance(j, int):
            out += (j // weight) % 2 * step
        else:
            out = out + lax.rem(lax.div(j, weight), 2) * step
    return out


def reduce_all(groups, n_dp, xs, parts):
    plans = []
    for source, start, n, rounds, gather in parts:
        if gather:
            steps = [n >> (k + 1) for k in range(len(rounds))]
        else:
            steps = [b * groups if a == "dp" else b for a, b in rounds]
        bases = functools.partial(bit_place, steps)
        plans.append((rounds, bases, gather, source, start, n))
    shapes = [(p[5],) + xs[p[3]].shape[1:] for p in plans]
    most = max(len(p[0]) for p in plans)
    peers = [("dp", b) for b in bits_of(n_dp)] + [("group", b) for b in bits_of(groups)]
    sems = pltpu.SemaphoreType.DMA((len(plans), most))
    return pl.pallas_call(
        functools.partial(reduce_kernel, plans, len(xs), peers),
        out_shape=tuple(
            jax.ShapeDtypeStruct(shape, BF16) if p[2] else jax.ShapeDtypeStruct((1,) + shape[1:], F32)
            for shape, p in zip(shapes, plans)),
        in_specs=[VMEM] * len(xs),
        out_specs=(VMEM,) * len(plans),
        scratch_shapes=[pltpu.VMEM((s[0] // 2,) + s[1:], F32) for s in shapes]
        + [pltpu.VMEM(s, BF16) for s in shapes] * 2 + [sems] * 4,
        compiler_params=pltpu.CompilerParams(
            collective_id=1, has_side_effects=True, vmem_limit_bytes=48 << 20),
        name="reduce_all",
    )(*xs)


def per_device(queries, item_features, corpus, sample_ids, sample_shift, w1, w2):
    groups = lax.axis_size("group")
    member = lax.axis_index("group")
    n_dp = lax.axis_size("dp")
    d = lax.axis_index("dp")
    query_rows, emb = queries.shape
    quota = query_rows // groups
    negs = sample_ids.shape[0] // groups
    rows = quota + negs
    fg = item_features.shape[1]
    scale = emb ** (-0.5)

    def shift(x, s):
        return lax.ppermute(x, "group", [(i, (i + s) % groups) for i in range(groups)])

    def at(x, i):
        return lax.dynamic_index_in_dim(x, lax.rem(i, groups), 0, keepdims=False)

    def place_columns(parts):
        if groups == 2:
            swap = member == 0
            return jnp.concatenate(
                [jnp.where(swap, parts[0], parts[1]), jnp.where(swap, parts[1], parts[0])], 1)
        out = jnp.zeros((parts[0].shape[0], groups * fg), BF16)
        for s in range(groups):
            start = lax.rem(member + groups - s, groups) * fg
            out = lax.dynamic_update_slice_in_dim(out, parts[s], start, 1)
        return out

    q_all = lax.all_gather(queries, "dp", axis=0, tiled=True)

    def swap_dp(x, step):
        return lax.ppermute(x, "dp", [(i, i ^ step) for i in range(n_dp)])

    quarter = lax.rem(d, 4)
    odd, high = lax.rem(quarter, 2) == 1, quarter >= 2
    w1_rows, w2_rows = w1.shape[0] // 4, w2.shape[0] // 4
    piece = jnp.concatenate([
        lax.dynamic_slice_in_dim(w1, quarter * w1_rows, w1_rows),
        lax.dynamic_slice_in_dim(w2, quarter * w2_rows, w2_rows).reshape(-1, w1.shape[1]),
    ], 0)
    items = item_features.reshape(groups, quota, fg)
    sample_ids, piece = lax.optimization_barrier((sample_ids, piece))
    got = [shift(piece, s) for s in range(1, groups)]
    ids = sample_ids.reshape(groups, negs)
    item_parts = [shift(at(items, member + s), s) for s in range(1, groups)]
    far_rows = [
        corpus.at[at(ids, member + s)].get(mode="promise_in_bounds") for s in range(1, groups)
    ]
    picked_parts = [shift(far_rows[s - 1], s) for s in range(1, groups)]
    own_ids, _ = lax.optimization_barrier((at(ids, member), far_rows))
    own_rows = corpus.at[own_ids].get(mode="promise_in_bounds")
    blocks = [jnp.concatenate([at(items, member), own_rows], 0)]
    for s in range(1, groups):
        blocks.append(jnp.concatenate([at(items, member + s), far_rows[s - 1]], 0))
    local = jnp.stack(blocks[:1] if groups == 2 else blocks)

    w1s, w2s = [w1], [w2]
    for p0 in got:
        p2 = swap_dp(p0, 2)
        p1, p3 = swap_dp(p0, 1), swap_dp(p2, 1)
        low = [jnp.where(odd, p1, p0), jnp.where(odd, p0, p1)]
        upp = [jnp.where(odd, p3, p2), jnp.where(odd, p2, p3)]
        placed = [jnp.where(high, u, l) for u, l in zip(upp, low)]
        placed += [jnp.where(high, l, u) for u, l in zip(upp, low)]
        w1s.append(jnp.concatenate([p[:w1_rows] for p in placed], 0))
        w2s.append(jnp.concatenate([p[w1_rows:].reshape(-1, emb) for p in placed], 0))

    feats = place_columns(
        blocks[:1]
        + [jnp.concatenate([a, b], 0) for a, b in zip(item_parts, picked_parts)]
    )

    embedded = jnp.zeros((rows, emb), F32)
    pre_own = None
    for s in range(groups):
        pre = mm(feats, w1s[s])
        hid = jnp.maximum(pre, 0.0).astype(BF16)
        if s == 0:
            pre_own, hid_own = pre, hid
        embedded = embedded + mm(hid, w2s[s])
    inverse = lax.rsqrt(jnp.mean(embedded * embedded, -1, keepdims=True) + 1e-06)
    normed = (embedded * inverse).astype(BF16)
    shift_own = lax.dynamic_slice_in_dim(sample_shift, member * negs, negs).astype(F32)
    bias = jnp.concatenate([jnp.zeros((quota,), F32), -shift_own])

    log_total, grad_hat, query_part, landed = score(
        groups, n_dp, local, q_all, normed, bias[:, None])
    log_total = log_total.reshape(-1)
    rest = place_columns(
        [jnp.concatenate(blocks[1:], 0)] + [landed[s - 1].reshape(-1, fg) for s in range(1, groups)]
    )

    query_own = lax.dynamic_slice_in_dim(queries, member * quota, quota).astype(F32)
    positive_own = normed[:quota].astype(F32)
    positive = scale * jnp.sum(query_own * positive_own, -1)
    query_loss = (
        lax.dynamic_slice_in_dim(log_total, d * query_rows + member * quota, quota) - positive
    )
    target = jnp.concatenate([query_own, jnp.zeros((negs, emb), F32)], 0)
    grad_normed = scale * (grad_hat - target)
    along = jnp.sum(grad_normed * embedded, -1, keepdims=True)
    grad_embed = (
        inverse * grad_normed - inverse**3 * embedded * along / emb
    ).astype(BF16)

    pre_rest = mm(rest, w1)
    hid_rest = jnp.maximum(pre_rest, 0.0).astype(BF16)
    back = jnp.concatenate(
        [grad_embed] + [shift(grad_embed, (groups - t) % groups) for t in range(1, groups)], 0
    )
    mask = jnp.concatenate([pre_own, pre_rest], 0) > 0
    grad_pre = jnp.where(mask, mm(back, w2.T), 0.0).astype(BF16)
    hid_all = jnp.concatenate([hid_own, hid_rest], 0)
    over_rows = (((0,), (0,)), ((), ()))
    grad_w2 = lax.dot_general(hid_all, back, over_rows, preferred_element_type=F32)
    feats_all = jnp.concatenate([feats, rest], 0)
    grad_w1 = lax.dot_general(feats_all, grad_pre, over_rows, preferred_element_type=F32)
    dp_bits = bits_of(n_dp)
    near, far = dp_bits[:1], dp_bits[:1:-1]
    along_first = [("dp", b) for b in near + dp_bits[1:2] + far]
    along_last = [("dp", b) for b in near + far + dp_bits[1:2]]
    query_order = (
        [("dp", near[0])]
        + [("group", b) for b in bits_of(groups)]
        + [("dp", b) for b in dp_bits[1:2] + far]
    )
    pad = -grad_w2.shape[0] % (16 * n_dp)
    padded = jnp.pad(grad_w2, ((0, pad), (0, 0)))
    xs = [
        grad_w1.reshape(2 * n_dp, -1, grad_w1.shape[1]),
        padded.reshape(n_dp, -1, emb),
        query_part.reshape(n_dp * groups, quota, emb),
    ]
    out_a, out_b, out_w2, query_sum = reduce_all(groups, n_dp, xs, [
        (0, 0, n_dp, along_last, True),
        (0, n_dp, n_dp, along_first, True),
        (1, 0, n_dp, along_first, True),
        (2, 0, n_dp * groups, query_order, False),
    ])
    grad_query = scale * (query_sum[0] - positive_own)
    grad_w1 = jnp.concatenate([out_a, out_b], 0).reshape(grad_w1.shape).astype(F32)
    grad_w2 = out_w2.reshape(padded.shape)[: grad_w2.shape[0]].astype(F32)
    return (query_loss, grad_query, grad_w1, grad_w2)


def solution(mesh):
    in_specs = (
        P("dp", None),
        P("dp", "group"),
        P("dp", "group"),
        P("dp"),
        P("dp"),
        P(None, "group"),
        P("group", None),
    )
    out_specs = (P(("dp", "group")), P(("dp", "group"), None), P(None, "group"), P("group", None))
    return jax.shard_map(
        per_device, mesh=mesh, in_specs=in_specs, out_specs=out_specs, check_vma=False
    )
```

```python
import functools

import jax
import jax.numpy as jnp
from jax import lax
from jax.experimental import pallas as pl
from jax.experimental.pallas import tpu as pltpu
from jax.sharding import PartitionSpec as P

F32 = jnp.float32
BF16 = jnp.bfloat16
MESH = pl.DeviceIdType.MESH
ANY = pl.BlockSpec(memory_space=pl.ANY)
VMEM = pl.BlockSpec(memory_space=pltpu.VMEM)


def mm(a, b):
    return jnp.dot(a, b, preferred_element_type=F32)


def bits_of(n):
    return [1 << i for i in range(n.bit_length() - 1)]


def partner(axis, step):
    i = lax.axis_index(axis)
    bit = lax.rem(lax.div(i, step), 2)
    return bit, {axis: i + step - 2 * step * bit}


def greet(peers):
    barrier = pltpu.get_barrier_semaphore()
    for peer in peers:
        pl.semaphore_signal(barrier, inc=1, device_id=peer, device_id_type=MESH)
    pl.semaphore_wait(barrier, len(peers))


def score_kernel(groups, n_dp, local, queries_in, normed, normed_t, bias,
                 total_ref, hat_ref, part_ref, rest_ref,
                 queries, logits, stats, arrived, qsem, send_sem, recv_sem, fsend, frecv):
    tiles, cols, width = logits.shape
    emb = normed.shape[1]
    scale = emb ** (-0.5)
    member = lax.axis_index("group")
    rounds = [("dp", b) for b in bits_of(n_dp)] + [("group", b) for b in bits_of(groups)]
    peers = [partner(a, b)[1] for a, b in rounds]
    others = [lax.rem(member + s, groups) for s in range(1, groups)]
    extra = [{"group": o} for o in others] if groups > 2 else []
    fetch = pltpu.make_async_copy(queries_in, queries, qsem)
    fetch.start()
    greet(peers + extra)
    copies = []
    for s in range(1, groups):
        for t in range(1, groups):
            k = (s - 1) * (groups - 1) + t - 1
            copy = pltpu.make_async_remote_copy(
                src_ref=local.at[(s + t) % groups],
                dst_ref=rest_ref.at[s - 1, t - 1],
                send_sem=fsend.at[k], recv_sem=frecv.at[k],
                device_id={"group": others[s - 1]}, device_id_type=MESH)
            copy.start()
            copies.append(copy)

    def first(i, carry):
        q = queries[pl.ds(pl.multiple_of(i * width, width), width), :]
        block = scale * lax.dot_general(
            normed[...], q, (((1,), (1,)), ((), ())), preferred_element_type=F32) + bias[...]
        logits[i] = block
        top = jnp.max(block, 0, keepdims=True)
        stats[0, 0, pl.ds(i, 1), :] = top
        stats[0, 1, pl.ds(i, 1), :] = jnp.sum(jnp.exp(block - top), 0, keepdims=True)
        return carry

    fetch.wait()
    lax.fori_loop(0, tiles, first, 0)
    for r, peer in enumerate(peers):
        copy = pltpu.make_async_remote_copy(
            src_ref=stats.at[r], dst_ref=arrived.at[r],
            send_sem=send_sem.at[r], recv_sem=recv_sem.at[r],
            device_id=peer, device_id_type=MESH)
        copy.start()
        copy.wait()
        m0, s0, m1, s1 = stats[r, 0], stats[r, 1], arrived[r, 0], arrived[r, 1]
        top = jnp.maximum(m0, m1)
        stats[r + 1, 0] = top
        stats[r + 1, 1] = s0 * jnp.exp(m0 - top) + s1 * jnp.exp(m1 - top)
    last = len(peers)
    total_ref[...] = stats[last, 0] + jnp.log(stats[last, 1])
    hat_ref[...] = jnp.zeros_like(hat_ref)

    def second(i, carry):
        at_i = pl.ds(pl.multiple_of(i * width, width), width)
        p = jnp.exp(logits[i] - total_ref[pl.ds(i, 1), :]).astype(BF16)
        hat_ref[...] += mm(p, queries[at_i, :])
        part_ref[at_i, :] = mm(normed_t[...], p).T
        return carry

    lax.fori_loop(0, tiles, second, 0)
    for copy in copies:
        copy.wait()


def score(groups, n_dp, local, queries, normed, bias):
    rows, fg = local.shape[1:]
    width = 256
    total, emb = queries.shape
    tiles = total // width
    rounds = len(bits_of(n_dp)) + len(bits_of(groups))
    n_copies = (groups - 1) ** 2
    return pl.pallas_call(
        functools.partial(score_kernel, groups, n_dp),
        out_shape=(
            jax.ShapeDtypeStruct((tiles, width), F32),
            jax.ShapeDtypeStruct((rows, emb), F32),
            jax.ShapeDtypeStruct((total, emb), F32),
            jax.ShapeDtypeStruct((groups - 1, groups - 1, rows, fg), BF16),
        ),
        in_specs=[ANY, ANY, VMEM, VMEM, VMEM],
        out_specs=(VMEM, VMEM, VMEM, ANY),
        scratch_shapes=[
            pltpu.VMEM((total, emb), BF16),
            pltpu.VMEM((tiles, rows, width), F32),
            pltpu.VMEM((rounds + 1, 2, tiles, width), F32),
            pltpu.VMEM((rounds, 2, tiles, width), F32),
            pltpu.SemaphoreType.DMA,
            pltpu.SemaphoreType.DMA((rounds,)),
            pltpu.SemaphoreType.DMA((rounds,)),
            pltpu.SemaphoreType.DMA((n_copies,)),
            pltpu.SemaphoreType.DMA((n_copies,)),
        ],
        compiler_params=pltpu.CompilerParams(
            collective_id=0, has_side_effects=True, vmem_limit_bytes=44 << 20),
        name="score",
    )(local, queries, normed, normed.T, bias)


def reduce_kernel(plans, n_in, n_peers_of, *refs):
    n = len(plans)
    ins, refs = refs[:n_in], refs[n_in:]
    outs = refs[:n]
    accs, sends, recvs = (refs[n + i * n : 2 * n + i * n] for i in range(3))
    send_sem, recv_sem, gsend, grecv = refs[4 * n :]
    greet([partner(a, b)[1] for a, b in n_peers_of])
    live = {}

    def begin(i, r):
        rounds, bases, _, source, start, count = plans[i]
        bit, peer = partner(*rounds[r])
        half = count >> (r + 1)
        at0 = count - 2 * half

        def stage(j, carry):
            if r == 0:
                block = ins[source][start + bases(j) + (1 - bit) * bases(half)]
            else:
                block = accs[i][(1 - bit) * half + j]
            sends[i][at0 + j] = block.astype(BF16)
            return carry

        lax.fori_loop(0, half, stage, 0)
        copy = pltpu.make_async_remote_copy(
            src_ref=sends[i].at[pl.ds(at0, half)], dst_ref=recvs[i].at[pl.ds(at0, half)],
            send_sem=send_sem.at[i, r], recv_sem=recv_sem.at[i, r],
            device_id=peer, device_id_type=MESH)
        copy.start()
        live[i] = copy

    def finish(i, r):
        rounds, bases, _, source, start, count = plans[i]
        bit, _ = partner(*rounds[r])
        half = count >> (r + 1)
        at0 = count - 2 * half
        live[i].wait()

        def add(j, carry):
            if r == 0:
                block = ins[source][start + bases(j) + bit * bases(half)]
            else:
                block = accs[i][bit * half + j]
            accs[i][j] = block + recvs[i][at0 + j].astype(F32)
            return carry

        lax.fori_loop(0, half, add, 0)

    def place(i, r):
        rounds = plans[i][0]
        return sum(partner(*rounds[k])[0] * (plans[i][5] >> (k + 1)) for k in range(r + 1))

    def share(i, r):
        peer = partner(*plans[i][0][r])[1]
        span = pl.ds(place(i, r), plans[i][5] >> (r + 1))
        copy = pltpu.make_async_remote_copy(
            src_ref=outs[i].at[span], dst_ref=outs[i].at[span],
            send_sem=gsend.at[i, r], recv_sem=grecv.at[i, r],
            device_id=peer, device_id_type=MESH)
        copy.start()
        live[i] = copy

    def advance(i, step):
        rounds, _, gather = plans[i][:3]
        k = len(rounds)
        if 0 < step <= k:
            finish(i, step - 1)
        if step < k:
            begin(i, step)
        elif step == k and not gather:
            outs[i][0] = accs[i][0]
        elif gather and step <= 2 * k:
            if step == k:
                outs[i][place(i, k - 1)] = accs[i][0].astype(BF16)
            else:
                live[i].wait()
            if step < 2 * k:
                share(i, 2 * k - 1 - step)

    steps = max(len(p[0]) * (2 if p[2] else 1) for p in plans) + 1
    for step in range(steps):
        for i in range(n):
            advance(i, step)


def bit_place(steps, j):
    k = len(steps)
    out = 0
    for i, step in enumerate(steps):
        weight = 1 << (k - 1 - i)
        if isinstance(j, int):
            out += (j // weight) % 2 * step
        else:
            out = out + lax.rem(lax.div(j, weight), 2) * step
    return out


def reduce_all(groups, n_dp, xs, parts):
    plans = []
    for source, start, n, rounds, gather in parts:
        if gather:
            steps = [n >> (k + 1) for k in range(len(rounds))]
        else:
            steps = [b * groups if a == "dp" else b for a, b in rounds]
        bases = functools.partial(bit_place, steps)
        plans.append((rounds, bases, gather, source, start, n))
    shapes = [(p[5],) + xs[p[3]].shape[1:] for p in plans]
    most = max(len(p[0]) for p in plans)
    peers = [("dp", b) for b in bits_of(n_dp)] + [("group", b) for b in bits_of(groups)]
    sems = pltpu.SemaphoreType.DMA((len(plans), most))
    return pl.pallas_call(
        functools.partial(reduce_kernel, plans, len(xs), peers),
        out_shape=tuple(
            jax.ShapeDtypeStruct(shape, BF16) if p[2] else jax.ShapeDtypeStruct((1,) + shape[1:], F32)
            for shape, p in zip(shapes, plans)),
        in_specs=[VMEM] * len(xs),
        out_specs=(VMEM,) * len(plans),
        scratch_shapes=[pltpu.VMEM((s[0] // 2,) + s[1:], F32) for s in shapes]
        + [pltpu.VMEM(s, BF16) for s in shapes] * 2 + [sems] * 4,
        compiler_params=pltpu.CompilerParams(
            collective_id=1, has_side_effects=True, vmem_limit_bytes=48 << 20),
        name="reduce_all",
    )(*xs)


def per_device(queries, item_features, corpus, sample_ids, sample_shift, w1, w2):
    groups = lax.axis_size("group")
    member = lax.axis_index("group")
    n_dp = lax.axis_size("dp")
    d = lax.axis_index("dp")
    query_rows, emb = queries.shape
    quota = query_rows // groups
    negs = sample_ids.shape[0] // groups
    rows = quota + negs
    fg = item_features.shape[1]
    scale = emb ** (-0.5)

    def shift(x, s):
        return lax.ppermute(x, "group", [(i, (i + s) % groups) for i in range(groups)])

    def at(x, i):
        return lax.dynamic_index_in_dim(x, lax.rem(i, groups), 0, keepdims=False)

    def place_columns(parts):
        if groups == 2:
            swap = member == 0
            return jnp.concatenate(
                [jnp.where(swap, parts[0], parts[1]), jnp.where(swap, parts[1], parts[0])], 1)
        out = jnp.zeros((parts[0].shape[0], groups * fg), BF16)
        for s in range(groups):
            start = lax.rem(member + groups - s, groups) * fg
            out = lax.dynamic_update_slice_in_dim(out, parts[s], start, 1)
        return out

    q_all = lax.all_gather(queries, "dp", axis=0, tiled=True)

    def swap_dp(x, step):
        return lax.ppermute(x, "dp", [(i, i ^ step) for i in range(n_dp)])

    def beside(x, cols):
        if x.shape[1] <= cols:
            return jnp.concatenate(jnp.split(x, cols // x.shape[1], 0), 1)
        return jnp.concatenate(jnp.split(x, x.shape[1] // cols, 1), 0)

    def restored(x, cols):
        if cols <= x.shape[1]:
            return jnp.concatenate(jnp.split(x, x.shape[1] // cols, 1), 0)
        return jnp.concatenate(jnp.split(x, cols // x.shape[1], 0), 1)

    quarter = lax.rem(d, 4)
    odd, high = lax.rem(quarter, 2) == 1, quarter >= 2
    w1_rows, w2_rows = w1.shape[0] // 4, w2.shape[0] // 4
    piece = jnp.concatenate([
        lax.dynamic_slice_in_dim(w1, quarter * w1_rows, w1_rows),
        beside(lax.dynamic_slice_in_dim(w2, quarter * w2_rows, w2_rows), w1.shape[1]),
    ], 0)
    items = item_features.reshape(groups, quota, fg)
    sample_ids, piece = lax.optimization_barrier((sample_ids, piece))
    got = [shift(piece, s) for s in range(1, groups)]
    ids = sample_ids.reshape(groups, negs)
    far_rows = [
        corpus.at[at(ids, member + s)].get(mode="promise_in_bounds") for s in range(1, groups)
    ]
    far_rows, items, got = lax.optimization_barrier((far_rows, items, got))
    item_parts = [shift(at(items, member + s), s) for s in range(1, groups)]
    picked_parts = [shift(far_rows[s - 1], s) for s in range(1, groups)]
    own_rows = corpus.at[at(ids, member)].get(mode="promise_in_bounds")
    blocks = [jnp.concatenate([at(items, member), own_rows], 0)]
    for s in range(1, groups):
        blocks.append(jnp.concatenate([at(items, member + s), far_rows[s - 1]], 0))
    local = jnp.stack(blocks[:1] if groups == 2 else blocks)

    w1s, w2s = [w1], [w2]
    for p0 in got:
        p2 = swap_dp(p0, 2)
        p1, p3 = swap_dp(p0, 1), swap_dp(p2, 1)
        low = [jnp.where(odd, p1, p0), jnp.where(odd, p0, p1)]
        upp = [jnp.where(odd, p3, p2), jnp.where(odd, p2, p3)]
        placed = [jnp.where(high, u, l) for u, l in zip(upp, low)]
        placed += [jnp.where(high, l, u) for u, l in zip(upp, low)]
        w1s.append(jnp.concatenate([p[:w1_rows] for p in placed], 0))
        w2s.append(jnp.concatenate([restored(p[w1_rows:], emb) for p in placed], 0))

    feats = place_columns(
        blocks[:1]
        + [jnp.concatenate([a, b], 0) for a, b in zip(item_parts, picked_parts)]
    )

    embedded = jnp.zeros((rows, emb), F32)
    pre_own = None
    for s in range(groups):
        pre = mm(feats, w1s[s])
        hid = jnp.maximum(pre, 0.0).astype(BF16)
        if s == 0:
            pre_own, hid_own = pre, hid
        embedded = embedded + mm(hid, w2s[s])
    inverse = lax.rsqrt(jnp.mean(embedded * embedded, -1, keepdims=True) + 1e-06)
    normed = (embedded * inverse).astype(BF16)
    shift_own = lax.dynamic_slice_in_dim(sample_shift, member * negs, negs).astype(F32)
    bias = jnp.concatenate([jnp.zeros((quota,), F32), -shift_own])

    log_total, grad_hat, query_part, landed = score(
        groups, n_dp, local, q_all, normed, bias[:, None])
    log_total = log_total.reshape(-1)
    rest = place_columns(
        [jnp.concatenate(blocks[1:], 0)] + [landed[s - 1].reshape(-1, fg) for s in range(1, groups)]
    )

    query_own = lax.dynamic_slice_in_dim(queries, member * quota, quota).astype(F32)
    positive_own = normed[:quota].astype(F32)
    positive = scale * jnp.sum(query_own * positive_own, -1)
    query_loss = (
        lax.dynamic_slice_in_dim(log_total, d * query_rows + member * quota, quota) - positive
    )
    target = jnp.concatenate([query_own, jnp.zeros((negs, emb), F32)], 0)
    grad_normed = scale * (grad_hat - target)
    along = jnp.sum(grad_normed * embedded, -1, keepdims=True)
    grad_embed = (
        inverse * grad_normed - inverse**3 * embedded * along / emb
    ).astype(BF16)

    pre_rest = mm(rest, w1)
    hid_rest = jnp.maximum(pre_rest, 0.0).astype(BF16)
    back = jnp.concatenate(
        [grad_embed] + [shift(grad_embed, (groups - t) % groups) for t in range(1, groups)], 0
    )
    mask = jnp.concatenate([pre_own, pre_rest], 0) > 0
    grad_pre = jnp.where(mask, mm(back, w2.T), 0.0).astype(BF16)
    hid_all = jnp.concatenate([hid_own, hid_rest], 0)
    over_rows = (((0,), (0,)), ((), ()))
    grad_w2 = lax.dot_general(hid_all, back, over_rows, preferred_element_type=F32)
    feats_all = jnp.concatenate([feats, rest], 0)
    grad_w1 = lax.dot_general(feats_all, grad_pre, over_rows, preferred_element_type=F32)
    dp_bits = bits_of(n_dp)
    near, far = dp_bits[:1], dp_bits[:1:-1]
    along_first = [("dp", b) for b in near + dp_bits[1:2] + far]
    along_last = [("dp", b) for b in near + far + dp_bits[1:2]]
    query_order = (
        [("dp", near[0])]
        + [("group", b) for b in bits_of(groups)]
        + [("dp", b) for b in dp_bits[1:2] + far]
    )
    pad = -grad_w2.shape[0] % (16 * n_dp)
    padded = jnp.pad(grad_w2, ((0, pad), (0, 0)))
    xs = [
        grad_w1.reshape(2 * n_dp, -1, grad_w1.shape[1]),
        padded.reshape(n_dp, -1, emb),
        query_part.reshape(n_dp * groups, quota, emb),
    ]
    out_a, out_b, out_w2, query_sum = reduce_all(groups, n_dp, xs, [
        (0, 0, n_dp, along_last, True),
        (0, n_dp, n_dp, along_first, True),
        (1, 0, n_dp, along_first, True),
        (2, 0, n_dp * groups, query_order, False),
    ])
    grad_query = scale * (query_sum[0] - positive_own)
    grad_w1 = jnp.concatenate([out_a, out_b], 0).reshape(grad_w1.shape).astype(F32)
    grad_w2 = out_w2.reshape(padded.shape)[: grad_w2.shape[0]].astype(F32)
    return (query_loss, grad_query, grad_w1, grad_w2)


def solution(mesh):
    in_specs = (
        P("dp", None),
        P("dp", "group"),
        P("dp", "group"),
        P("dp"),
        P("dp"),
        P(None, "group"),
        P("group", None),
    )
    out_specs = (P(("dp", "group")), P(("dp", "group"), None), P(None, "group"), P("group", None))
    return jax.shard_map(
        per_device, mesh=mesh, in_specs=in_specs, out_specs=out_specs, check_vma=False
    )
```
